256 devices in a mesh: dp: 8 (over y, z_lo), expert: 32 (over z_hi, x, core).
Axes of the slice: x: 4, y: 4, z: 8 (z_hi: 4, z_lo: 2; z = z_hi * 2 + z_lo), core: 2. Of those that a mesh axis runs over, the one named last changes fastest.
Arguments:
- tokens: bfloat16 [32768, 2048], P(('dp', 'expert')), may hold values from -6 to 6
- cotangent: bfloat16 [32768, 2048], P(('dp', 'expert')), may hold values from -6 to 6
- routes: int32 [32768, 4], P(('dp', 'expert')), may hold values from 0 to 31, all different within a row; in each aligned block of 128 rows (0 to 127, 128 to 255, ...) at most 17 rows name the same one
- gates: float32 [32768, 4], P(('dp', 'expert')), may hold values from 0.1 to 1
- w_gate: bfloat16 [32, 2048, 768], P('expert'), may hold values from -0.125 to 0.125
- w_up: bfloat16 [32, 2048, 768], P('expert'), may hold values from -0.125 to 0.125
- w_down: bfloat16 [32, 768, 2048], P('expert'), may hold values from -0.21875 to 0.21875
Outputs:
- token_grad: bfloat16 [32768, 2048], P(('dp', 'expert'))
- gate_grad: float32 [32, 2048, 768], P('expert', None, 'dp')
- up_grad: float32 [32, 2048, 768], P('expert', None, 'dp')
- down_grad: float32 [32, 768, 2048], P('expert', 'dp')
The draws below stay inside these ranges and needn't reach their ends.
Inputs may be any that keep to these rules, and one draw needn't show every extreme that they name: `routes`: each row names 4 different experts. Within the rows of one device no expert is named by more than 17 rows, a bound that some block reaches.
All inputs are finite; a program needn't handle non-finite values.
Results may differ from the reference program's by a relative error of at most 0.015.
Values may be sent and summed in bfloat16 or wider, within the bound.
A program may use at most 128 MiB of HBM per device.

```python
import math
import jax
import jax.numpy as jnp
import numpy as np
from jax import lax

D = 2048
H = 768
TOP = 4
TOK_DEV = 128
EXPERTS = 32
CAP = 17
TOKENS = 32768
N_DP = 8
N_EXPERT = 32


def block_levels(rng, dims, cuts, least, largest):
    gain = 1.0
    for dim, blocks in cuts:
        steps = jax.random.uniform(jax.random.fold_in(jax.random.fold_in(rng, 6), dim), (blocks,), jnp.float32, least / len(cuts), largest / len(cuts))
        gain = gain * jnp.repeat(jnp.exp(steps), dims[dim] // blocks).reshape((-1,) + (1,) * (len(dims) - 1 - dim))
    return gain


def deal_out(rng, own, number, rows, count, top, reach, skew):
    ranking = jax.random.permutation(rng, count)
    heavy_load, usual = shares(count, rows * top, reach, skew, True), shares(count, rows * top, reach, skew, False)
    places = jnp.arange(count)

    def named(tallies, rotation):
        used = int((tallies > 0).sum())
        fixed = max(1, used // 4)
        moved = fixed + (places - fixed + rotation * (used - fixed)) % max(1, count - fixed)
        return jnp.zeros((count,), jnp.int32).at[ranking[jnp.where(places < fixed, places, moved)]].set(jnp.asarray(tallies, jnp.int32))

    tallies = jnp.where(number % 4 == 0, named(heavy_load, number // 4), named(usual, number - number // 4 - 1))
    mixed = jax.random.permutation(jax.random.fold_in(own, 3), count)
    giver, receiver = mixed[0:count // 2 * 2:2], mixed[1:count // 2 * 2:2]
    margin = jnp.minimum(tallies[giver] - 1, reach - tallies[receiver]) // 2
    margin = jnp.where((giver == ranking[0]) | (receiver == ranking[0]) | (tallies[receiver] == 0), 0, jnp.maximum(margin, 0))
    moved = jax.random.randint(jax.random.fold_in(own, 4), (count // 2,), 0, 1 << 20) % (margin + 1)
    tallies = tallies.at[giver].add(-moved).at[receiver].add(moved)
    members = jnp.searchsorted(jnp.cumsum(tallies), jnp.arange(rows * top), side="right").astype(jnp.int32)
    listing = members.reshape(top, rows).T
    listing = listing[jax.random.permutation(jax.random.fold_in(own, 1), rows)]
    rotation = jax.random.randint(jax.random.fold_in(own, 2), (rows, 1), 0, top)
    return jnp.take_along_axis(listing, (jnp.arange(top)[None, :] + rotation) % top, axis=1)


def shares(amount, total, most, lean, full):
    loads = [(1 << 20) // math.isqrt(rank ** lean) + 1 for rank in range(1, amount + 1)]
    largest = most if full else min(most, max(-(-total // amount), total * loads[0] // sum(loads)))
    least = 1 if total - largest >= amount - 1 else 0
    counts, spare = [largest] + [least] * (amount - 1), total - largest - least * (amount - 1)
    while spare > 0:
        free = [i for i in range(1, amount) if counts[i] < largest] or [i for i in range(1, amount) if counts[i] < most]
        whole, left = sum([loads[i] for i in free]), spare
        for i in free:
            more = min(most - counts[i], max(1, left * loads[i] // whole), spare)
            counts[i] = counts[i] + more
            spare = spare - more
    return np.array(counts)


def centred(rng, dims, deviation, limit, pieces=(), held_as=jnp.bfloat16):
    entries = jax.random.normal(rng, dims, jnp.float32) * deviation
    if len(pieces) > 0:
        entries = block_levels(rng, dims, pieces, -0.22, 0.18) * entries
    return jnp.clip(entries, min=-limit, max=limit).astype(held_as)


def setup_inputs(seed: int = 0) -> dict:
    key_of = jax.random.split(jax.random.key(seed), 8)
    tokens = centred(key_of[0], (TOKENS, D), 1.0, 6.0, ((0, 256),))
    cotangent = centred(key_of[1], (TOKENS, D), 1.0, 6.0, ((0, 256),))
    routes_keys = jax.random.split(jax.random.fold_in(key_of[2], 1), TOKENS // TOK_DEV)
    routes_turns = jax.random.permutation(jax.random.fold_in(key_of[2], 3), TOKENS // TOK_DEV)
    routes = jax.vmap(lambda own, number: deal_out(jax.random.fold_in(key_of[2], 2), own, number, TOK_DEV, EXPERTS, TOP, CAP, 2))(routes_keys, routes_turns).reshape((TOKENS, TOP))
    gates = jnp.clip(jnp.exp(math.log(1.0) - 2.3025851 * jax.random.uniform(key_of[3], (TOKENS, TOP), jnp.float32) ** block_levels(key_of[3], (TOKENS, TOP), ((0, 256),), -0.2, 0.2)), 0.1, 1.0)
    w_gate = centred(key_of[4], (EXPERTS, D, H), D ** -0.5, 0.125, ((0, 32),))
    w_up = centred(key_of[5], (EXPERTS, D, H), D ** -0.5, 0.125, ((0, 32),))
    w_down = centred(key_of[6], (EXPERTS, H, D), H ** -0.5, 0.21875, ((0, 32),))
    return dict(tokens=tokens, cotangent=cotangent, routes=routes, gates=gates, w_gate=w_gate, w_up=w_up, w_down=w_down)


def positions(routes_block, experts, cap):
    flat = routes_block.reshape(-1)
    onehot = (flat[:, None] == jnp.arange(experts, dtype=jnp.int32)[None, :]).astype(jnp.int32)
    before = jnp.cumsum(onehot, axis=0) - onehot
    slot = jnp.sum(before * onehot, axis=1).astype(jnp.int32)
    return flat * cap + slot


def placing(routes_block, gates_block, experts, cap):
    dest = positions(routes_block, experts, cap)
    hits = (jnp.arange(experts * cap, dtype=jnp.int32)[:, None] == dest[None, :]).astype(jnp.float32)
    hits = hits.reshape(experts * cap, routes_block.shape[0], routes_block.shape[1])
    return jnp.sum(hits, axis=2), jnp.sum(hits * gates_block[None, :, :].astype(jnp.float32), axis=2)


def expert_backward(rows_in, rows_grad, gate_mat, up_mat, down_mat):
    pre_gate = jnp.dot(rows_in, gate_mat, preferred_element_type=jnp.float32)
    pre_up = jnp.dot(rows_in, up_mat, preferred_element_type=jnp.float32)
    sigma = jax.nn.sigmoid(pre_gate)
    act = pre_gate * sigma
    hidden = (act * pre_up).astype(jnp.bfloat16)
    d_hidden = lax.dot_general(rows_grad, down_mat, (((1,), (1,)), ((), ())), preferred_element_type=jnp.float32)
    down_part = lax.dot_general(hidden, rows_grad, (((0,), (0,)), ((), ())), preferred_element_type=jnp.float32)
    d_up = (d_hidden * act).astype(jnp.bfloat16)
    d_gate = (d_hidden * pre_up * sigma * (1.0 + pre_gate * (1.0 - sigma))).astype(jnp.bfloat16)
    gate_part = lax.dot_general(rows_in, d_gate, (((0,), (0,)), ((), ())), preferred_element_type=jnp.float32)
    up_part = lax.dot_general(rows_in, d_up, (((0,), (0,)), ((), ())), preferred_element_type=jnp.float32)
    back = lax.dot_general(d_gate, gate_mat, (((1,), (1,)), ((), ())), preferred_element_type=jnp.float32)
    back = back + lax.dot_general(d_up, up_mat, (((1,), (1,)), ((), ())), preferred_element_type=jnp.float32)
    return (back.astype(jnp.bfloat16), gate_part.astype(jnp.bfloat16),
            up_part.astype(jnp.bfloat16), down_part.astype(jnp.bfloat16))


def reference(tokens, cotangent, routes, gates, w_gate, w_up, w_down):
    high = lax.Precision.HIGHEST
    x_all = tokens.reshape(N_DP, N_EXPERT, TOK_DEV, D)
    g_all = cotangent.reshape(N_DP, N_EXPERT, TOK_DEV, D)
    r_all = routes.reshape(N_DP, N_EXPERT, TOK_DEV, TOP)
    s_all = gates.reshape(N_DP, N_EXPERT, TOK_DEV, TOP)

    def group_step(carry, group):
        x_grp, g_grp, r_grp, s_grp = group
        plain, scaled = jax.vmap(lambda a, b: placing(a, b, EXPERTS, CAP))(r_grp, s_grp)
        sent_x = jnp.einsum("set,std->sed", plain, x_grp.astype(jnp.float32), precision=high).astype(jnp.bfloat16)
        sent_g = jnp.einsum("set,std->sed", scaled, g_grp.astype(jnp.float32), precision=high).astype(jnp.bfloat16)
        rows_x = sent_x.reshape(N_EXPERT, EXPERTS, CAP, D).transpose(1, 0, 2, 3).reshape(EXPERTS, N_EXPERT * CAP, D)
        rows_g = sent_g.reshape(N_EXPERT, EXPERTS, CAP, D).transpose(1, 0, 2, 3).reshape(EXPERTS, N_EXPERT * CAP, D)
        back, gate_part, up_part, down_part = lax.map(lambda a: expert_backward(*a), (rows_x, rows_g, w_gate, w_up, w_down))
        back = back.reshape(EXPERTS, N_EXPERT, CAP, D).transpose(1, 0, 2, 3).reshape(N_EXPERT, EXPERTS * CAP, D)
        grad_x = jnp.einsum("set,sed->std", plain, back.astype(jnp.float32), precision=high).astype(jnp.bfloat16)
        total_gate, total_up, total_down = carry
        carry = (total_gate + gate_part.astype(jnp.float32), total_up + up_part.astype(jnp.float32),
                 total_down + down_part.astype(jnp.float32))
        return carry, grad_x

    start = (jnp.zeros((EXPERTS, D, H), jnp.float32), jnp.zeros((EXPERTS, D, H), jnp.float32),
             jnp.zeros((EXPERTS, H, D), jnp.float32))
    sums, grad_x = lax.scan(group_step, start, (x_all, g_all, r_all, s_all))
    return grad_x.reshape(TOKENS, D), sums[0], sums[1], sums[2]
```

```python
import jax
import jax.numpy as jnp
from jax import lax
from jax.experimental import pallas as pl
from jax.experimental.pallas import tpu as pltpu
from jax.sharding import PartitionSpec as P

MESH = pl.DeviceIdType.MESH
F32 = jnp.float32
BF16 = jnp.bfloat16

D = 2048
H = 768
TOP = 4
TOK = 128
CAP = 17
NB = 4
NE = 8
PAD = 80
ROWS = NE * PAD
NQ = 4
C = D // NQ
HY = H // 4
HZ = HY // 2


def dot(a, b, dims=((1,), (0,))):
    return lax.dot_general(a, b, (dims, ((), ())), preferred_element_type=F32)


def kernel(
    info_in, tok_in, cot_in, wg_in, wu_in, wd_in,
    tg_out, down_out, gate_out, up_out,
    info, blk, sel, sgate, snd, rows, wg, wu, wd, pg, pu, dh,
    ht, dgt, dut, dg, du, brow, trow, pw, ra, rb, zs, zr_buf,
    in_sem, w_sem, is_sem, ir_sem, zs_sem, zr_sem, xs_sem, xr_sem,
    bs_sem, br_sem, ts_sem, tr_sem, as_sem, ar_sem, ds_sem, rb_sem, ms_sem, mr_sem,
):
    dp, ex = lax.axis_index("dp"), lax.axis_index("expert")
    y, zl = lax.div(dp, 2), lax.rem(dp, 2)
    zh, xc = lax.div(ex, NE), lax.rem(ex, NE)
    sign = 1 - 2 * zl
    zh_next, zh_prev = lax.rem(zh + sign + 4, 4), lax.rem(zh - sign + 4, 4)

    def dev(y_, zl_, zh_, xc_):
        return (y_ * 2 + zl_, zh_ * NE + xc_)

    up = dev(y, 0, lax.rem(zh + 1, 4), xc)
    down = dev(y, 1, lax.rem(zh + 3, 4), xc)
    ahead = dev(y, zl, zh_next, xc)
    prev_same = dev(y, zl, zh_prev, xc)
    prev_other = dev(y, 1 - zl, zh_prev, xc)
    y_up = dev(lax.rem(y + 1, 4), zl, zh, xc)
    y_down = dev(lax.rem(y + 3, 4), zl, zh, xc)
    mate = dev(y, 1 - zl, zh, xc)

    def copy(src, dst, send, recv, where):
        return pltpu.make_async_remote_copy(
            src_ref=src, dst_ref=dst, send_sem=send, recv_sem=recv,
            device_id=where, device_id_type=MESH)

    def landed(ref, sem):
        pltpu.make_async_copy(ref, ref, sem).wait()

    loads = []
    for q in range(2 * NQ):
        src = tok_in if q < NQ else cot_in
        loads.append(pltpu.make_async_copy(
            src.at[:, pl.ds(C * (q % NQ), C)], blk.at[q, 0], in_sem.at[q]))
    wloads = [pltpu.make_async_copy(a.at[0], b, w_sem.at[i])
              for i, (a, b) in enumerate(((wg_in, wg), (wu_in, wu), (wd_in, wd)))]
    for load in loads:
        load.start()
    for load in wloads:
        load.start()
    info[0] = info_in[...]

    barrier = pltpu.get_barrier_semaphore()
    for where in (ahead, prev_same, prev_other, y_up, y_down, mate):
        pl.semaphore_signal(barrier, inc=1, device_id=where, device_id_type=MESH)

    def greet(i, carry):
        peer = lax.rem(xc + i, NE)
        pl.semaphore_signal(barrier, inc=1, device_id=dev(y, zl, zh, peer), device_id_type=MESH)
        return carry

    lax.fori_loop(1, NE, greet, 0)
    pl.semaphore_wait(barrier, 6 + NE - 1)

    def z_copy(ref, i, send, recv):
        if i == 0:
            return copy(ref.at[0], ref.at[1 + zl], send.at[0], recv.at[zl], up)
        if i == 1:
            return copy(ref.at[0], ref.at[2 - zl], send.at[1], recv.at[1 - zl], down)
        return copy(ref.at[2], ref.at[3], send.at[2], recv.at[2], ahead)

    def block_copy(q, i):
        return z_copy(blk.at[q], i, zs_sem.at[q], zr_sem.at[q])

    icopies = [z_copy(info, i, is_sem, ir_sem) for i in range(3)]
    icopies[0].start()
    icopies[1].start()
    for load in loads:
        load.wait()

    def send_own(q):
        block_copy(q, 0).start()
        block_copy(q, 1).start()

    for q in range(2):
        send_own(q)

    landed(info.at[2], ir_sem.at[1])
    icopies[2].start()
    landed(info.at[1], ir_sem.at[0])
    landed(info.at[3], ir_sem.at[2])

    before_mask = (lax.broadcasted_iota(jnp.int32, (TOK, TOK), 0)
                   < lax.broadcasted_iota(jnp.int32, (TOK, TOK), 1)).astype(F32).astype(BF16)
    expert = (lax.broadcasted_iota(jnp.int32, (NE, TOK), 0) + NE * zh).astype(F32)
    slot = lax.broadcasted_iota(jnp.int32, (PAD, TOK), 0).astype(F32)
    scales = [jnp.zeros((PAD, 1), F32) for _ in range(NE)]
    for b in range(NB):
        chosen = jnp.zeros((NE, TOK), F32)
        weight = jnp.zeros((NE, TOK), F32)
        for k in range(TOP):
            hit = info[b, k:k + 1, :] == expert
            chosen = chosen + jnp.where(hit, 1.0, 0.0)
            weight = weight + jnp.where(hit, info[b, TOP + k:TOP + k + 1, :], 0.0)
        place = dot(chosen.astype(BF16), before_mask) + float(CAP * b)
        place = jnp.where(chosen > 0.0, place, -1.0)
        for j in range(NE):
            mine = jnp.where(slot == place[j:j + 1, :], 1.0, 0.0)
            sel[PAD * j:PAD * (j + 1), TOK * b:TOK * (b + 1)] = mine.astype(BF16)
            scales[j] = scales[j] + jnp.sum(mine * weight[j:j + 1, :], axis=1, keepdims=True)
    for j in range(NE):
        sgate[PAD * j:PAD * (j + 1), :] = jnp.broadcast_to(scales[j], (PAD, 128))

    pg[...] = jnp.zeros_like(pg)
    pu[...] = jnp.zeros_like(pu)
    dh[...] = jnp.zeros_like(dh)

    def spread(src, dst, send, recv):
        def one(i, carry):
            peer = lax.rem(xc + i, NE)
            copy(src.at[peer], dst.at[xc], send, recv, dev(y, zl, zh, peer)).start()
            return carry

        lax.fori_loop(1, NE, one, 0)

    def pick(q):
        block = blk.at[q]

        def part(n, carry):
            cols = pl.ds(pl.multiple_of(n * 256, 256), 256)
            got = dot(sel[...], block[:, :, cols].reshape(NB * TOK, 256))
            got = got * jnp.where(q >= NQ, sgate[:, 0:1], 1.0)
            snd[q, :, :, cols] = got.astype(BF16).reshape(NE, PAD, 256)
            return carry

        lax.fori_loop(0, C // 256, part, 0)
        spread(snd.at[q], rows.at[q], xs_sem.at[q], xr_sem.at[q])
        rows[q, xc] = snd[q, xc]

    def chunk_of(ref, q):
        return ref[q].reshape(ROWS, C)

    def forward(q):
        span = pl.ds(pl.multiple_of(q * C, C), C)

        def part(n, carry):
            cols = pl.ds(pl.multiple_of(n * 256, 256), 256)
            pg[:, cols] += dot(chunk_of(rows, q), wg[span, cols])
            pu[:, cols] += dot(chunk_of(rows, q), wu[span, cols])
            return carry

        lax.fori_loop(0, H // 256, part, 0)

    def activate():
        def part(n, carry):
            cols = pl.ds(pl.multiple_of(n * 128, 128), 128)
            pre, mul = pg[:, cols], pu[:, cols]
            sigma = jax.nn.sigmoid(pre)
            act = pre * sigma
            ht[cols, :] = jnp.transpose(act * mul).astype(BF16)
            pg[:, cols] = act
            pu[:, cols] = mul * sigma * (1.0 + pre * (1.0 - sigma))
            return carry

        lax.fori_loop(0, H // 128, part, 0)

    def backward(q):
        span = pl.ds(pl.multiple_of((q - NQ) * C, C), C)

        def part(n, carry):
            cols = pl.ds(pl.multiple_of(n * 256, 256), 256)
            dh[:, cols] += dot(chunk_of(rows, q), wd[cols, span], ((1,), (1,)))
            return carry

        lax.fori_loop(0, H // 256, part, 0)

    def stage(s, carry):
        @pl.when(s + 2 < 2 * NQ)
        def _():
            send_own(s + 2)

        @pl.when(s < 2 * NQ)
        def _():
            landed(blk.at[s, 2], zr_sem.at[s, 1])
            block_copy(s, 2).start()
            landed(blk.at[s, 1], zr_sem.at[s, 0])

        @pl.when((s >= 1) & (s < 2 * NQ + 1))
        def _():
            landed(blk.at[s - 1, 3], zr_sem.at[s - 1, 2])
            pick(s - 1)

        @pl.when(s >= 2)
        def _():
            q = s - 2
            landed(rows.at[q, pl.ds(0, NE - 1)], xr_sem.at[q])

            @pl.when(q < NQ)
            def _():
                forward(q)

            @pl.when(q == NQ - 1)
            def _():
                activate()

            @pl.when(q >= NQ)
            def _():
                backward(q)

        return carry

    for load in wloads:
        load.wait()
    lax.fori_loop(0, 2 * NQ + 2, stage, 0)

    def derive(n, carry):
        cols = pl.ds(pl.multiple_of(n * 128, 128), 128)
        grad = dh[:, cols]
        d_up = grad * pg[:, cols]
        d_gate = grad * pu[:, cols]
        du[:, cols] = d_up.astype(BF16)
        dg[:, cols] = d_gate.astype(BF16)
        dut[cols, :] = jnp.transpose(d_up).astype(BF16)
        dgt[cols, :] = jnp.transpose(d_gate).astype(BF16)
        return carry

    lax.fori_loop(0, H // 128, derive, 0)

    lefts = (ht, dgt, dut)
    firsts = (NQ, 0, 0)

    def partial(w, start, size, q):
        at = pl.ds(pl.multiple_of(start, 16), size)
        return dot(lefts[w][at, :], chunk_of(rows, firsts[w] + q))

    def partials(w, r):
        start = HY * lax.rem(y + r + 1, 4)

        def part(q, carry):
            cols = pl.ds(pl.multiple_of(q * C, C), C)
            pw[w, r, :, :, cols] = partial(w, start, HY, q).astype(BF16).reshape(2, HZ, C)
            return carry

        lax.fori_loop(0, NQ, part, 0)

    def far_copy(w, i):
        return copy(pw.at[w, 1, i], ra.at[w, i], as_sem.at[w, i], ar_sem.at[w, i],
                    y_down if i else y_up)

    def ring_copy(w, i, h):
        return copy(pw.at[w, 2 * i, h], rb.at[w, i, h], ds_sem.at[w, i, h], rb_sem.at[w, i, h],
                    y_down if i else y_up)

    for w in range(3):
        partials(w, 1)
        for i in range(2):
            far_copy(w, i).start()

    def sent(q, carry):
        landed(snd.at[q, pl.ds(0, NE - 1)], xs_sem.at[q])
        for i in range(3):
            block_copy(q, i).wait_send()
        return carry

    lax.fori_loop(0, 2 * NQ, sent, 0)
    for c in icopies:
        c.wait_send()

    def back(q, carry):
        def part(n, carry):
            at = pl.ds(pl.multiple_of(q * C + n * 256, 256), 256)
            cols = pl.ds(pl.multiple_of(n * 256, 256), 256)
            got = dot(dg[...], wg[at, :], ((1,), (1,))) + dot(du[...], wu[at, :], ((1,), (1,)))
            snd[q, :, :, cols] = got.astype(BF16).reshape(NE, PAD, 256)
            return carry

        lax.fori_loop(0, C // 256, part, 0)
        spread(snd.at[q], brow.at[q], bs_sem.at[q], br_sem.at[q])
        brow[q, xc] = snd[q, xc]
        return carry

    lax.fori_loop(0, NQ, back, 0)

    for w in range(3):
        partials(w, 0)
        partials(w, 2)
        for i in range(2):
            ring_copy(w, i, 1 - i).start()

    def t_copy(q, b):
        at = 2 if b == 3 else zl
        return copy(blk.at[q, b], trow.at[q, at], ts_sem.at[q, b - 1], tr_sem.at[q, at],
                    prev_other if b == 2 else prev_same)

    def combine(q):
        landed(brow.at[q, pl.ds(0, NE - 1)], br_sem.at[q])
        for b in (3, 1, 2, 0):
            got = dot(sel[:, TOK * b:TOK * (b + 1)], chunk_of(brow, q), ((0,), (0,)))
            if b:
                blk[q, b] = got.astype(BF16)
            else:
                pg[pl.ds(pl.multiple_of(q * TOK, TOK), TOK), 0:C] = got
            if b in (1, 3):
                t_copy(q, b).start()

    def pass_on(q):
        landed(trow.at[q, 2], tr_sem.at[q, 2])
        blk[q, 2] = (blk[q, 2].astype(F32) + trow[q, 2].astype(F32)).astype(BF16)
        t_copy(q, 2).start()

    def relay(w):
        for i in range(2):
            far_copy(w, i).wait_send()
            landed(ra.at[w, i], ar_sem.at[w, i])
            pw[w, 2 * i, i] = (pw[w, 2 * i, i].astype(F32) + ra[w, i].astype(F32)).astype(BF16)
            ring_copy(w, i, i).start()

    def return_step(q, carry):
        @pl.when(q < NQ)
        def _():
            combine(q)

        @pl.when(q >= 1)
        def _():
            pass_on(q - 1)

        @pl.when(q < 3)
        def _():
            relay(q)

        return carry

    lax.fori_loop(0, NQ + 1, return_step, 0)

    def finish_tokens(q, carry):
        landed(trow.at[q, 0], tr_sem.at[q, 0])
        landed(trow.at[q, 1], tr_sem.at[q, 1])
        cols = pl.ds(pl.multiple_of(q * C, C), C)
        total = pg[pl.ds(pl.multiple_of(q * TOK, TOK), TOK), 0:C]
        total = total + trow[q, 0].astype(F32) + trow[q, 1].astype(F32)
        tg_out[:, cols] = total.astype(BF16)
        for b in (1, 2, 3):
            t_copy(q, b).wait_send()
        return carry

    lax.fori_loop(0, NQ, finish_tokens, 0)

    outs = (down_out, gate_out, up_out)

    def mate_copy(w):
        return copy(zs.at[w], zr_buf.at[w], ms_sem.at[w], mr_sem.at[w], mate)

    def summed(w, half, q):
        cols = pl.ds(pl.multiple_of(q * C, C), C)
        own = partial(w, HY * y + HZ * half, HZ, q)
        return own + rb[w, 0, half, :, cols].astype(F32) + rb[w, 1, half, :, cols].astype(F32)

    for w in range(3):
        for i in range(2):
            for h in range(2):
                landed(rb.at[w, i, h], rb_sem.at[w, i, h])

        def give(q, carry):
            cols = pl.ds(pl.multiple_of(q * C, C), C)
            zs[w, :, cols] = summed(w, 1 - zl, q).astype(BF16)
            return carry

        lax.fori_loop(0, NQ, give, 0)
        mate_copy(w).start()

        def keep(q, carry):
            cols = pl.ds(pl.multiple_of(q * C, C), C)
            outs[w][:, cols] = summed(w, zl, q)
            return carry

        lax.fori_loop(0, NQ, keep, 0)

    for w in range(3):
        landed(zr_buf.at[w], mr_sem.at[w])
        outs[w][...] += zr_buf[w].astype(F32)
    for w in range(3):
        mate_copy(w).wait_send()
        for i in range(2):
            for h in range(2):
                ring_copy(w, i, h).wait_send()

    def back_sent(q, carry):
        landed(snd.at[q, pl.ds(0, NE - 1)], bs_sem.at[q])
        return carry

    lax.fori_loop(0, NQ, back_sent, 0)


def body(tokens, cotangent, routes, gates, w_gate, w_up, w_down):
    info = jnp.concatenate([routes.T.astype(F32), gates.T], axis=0)
    hbm = pl.BlockSpec(memory_space=pl.ANY)
    vmem = pl.BlockSpec(memory_space=pltpu.VMEM)
    V, S = pltpu.VMEM, pltpu.SemaphoreType.DMA
    token_grad, down, gate, up = pl.pallas_call(
        kernel,
        out_shape=(
            jax.ShapeDtypeStruct((TOK, D), BF16),
            jax.ShapeDtypeStruct((HZ, D), F32),
            jax.ShapeDtypeStruct((HZ, D), F32),
            jax.ShapeDtypeStruct((HZ, D), F32),
        ),
        in_specs=[vmem, hbm, hbm, hbm, hbm, hbm],
        out_specs=(vmem, vmem, vmem, vmem),
        scratch_shapes=[
            V((NB, 2 * TOP, TOK), F32),
            V((2 * NQ, NB, TOK, C), BF16),
            V((ROWS, NB * TOK), BF16),
            V((ROWS, 128), F32),
            V((2 * NQ, NE, PAD, C), BF16),
            V((2 * NQ, NE, PAD, C), BF16),
            V((D, H), BF16), V((D, H), BF16), V((H, D), BF16),
            V((ROWS, H), F32), V((ROWS, H), F32), V((ROWS, H), F32),
            V((H, ROWS), BF16), V((H, ROWS), BF16), V((H, ROWS), BF16),
            V((ROWS, H), BF16), V((ROWS, H), BF16),
            V((NQ, NE, PAD, C), BF16),
            V((NQ, 3, TOK, C), BF16),
            V((3, 3, 2, HZ, D), BF16),
            V((3, 2, HZ, D), BF16),
            V((3, 2, 2, HZ, D), BF16),
            V((3, HZ, D), BF16), V((3, HZ, D), BF16),
            S((2 * NQ,)), S((3,)), S((3,)), S((3,)),
            S((2 * NQ, 3)), S((2 * NQ, 3)), S((2 * NQ,)), S((2 * NQ,)),
            S((NQ,)), S((NQ,)), S((NQ, 3)), S((NQ, 3)),
            S((3, 2)), S((3, 2)), S((3, 2, 2)), S((3, 2, 2)), S((3,)), S((3,)),
        ],
        compiler_params=pltpu.CompilerParams(
            collective_id=0, has_side_effects=True, vmem_limit_bytes=62 * 1024 * 1024),
        cost_estimate=pl.CostEstimate(
            flops=8 * 2 * ROWS * D * H, bytes_accessed=16 * 1024 * 1024, transcendentals=ROWS * H),
    )(info, tokens, cotangent, w_gate, w_up, w_down)
    return token_grad, gate.T[None], up.T[None], down[None]


def solution(mesh):
    rows = P(("dp", "expert"), None)
    return jax.shard_map(
        body,
        mesh=mesh,
        in_specs=(rows, rows, rows, rows) + (P("expert", None, None),) * 3,
        out_specs=(rows, P("expert", None, "dp"), P("expert", None, "dp"), P("expert", "dp", None)),
        check_vma=False,
    )
```

```python
import jax
import jax.numpy as jnp
from jax import lax
from jax.experimental import pallas as pl
from jax.experimental.pallas import tpu as pltpu
from jax.sharding import PartitionSpec as P

MESH = pl.DeviceIdType.MESH
F32 = jnp.float32
BF16 = jnp.bfloat16

D = 2048
H = 768
TOP = 4
TOK = 128
CAP = 17
NB = 4
NE = 8
PAD = 80
ROWS = NE * PAD
NQ = 8
C = D // NQ
AHEAD = 4
NG = 4
GC = D // NG
NU = 3 * NG
HY = H // 4
HZ = HY // 2


def dot(a, b, dims=((1,), (0,))):
    return lax.dot_general(a, b, (dims, ((), ())), preferred_element_type=F32)


def kernel(
    routes_in, gates_in, tok_in, cot_in, wg_in, wu_in, wd_in,
    tg_out, down_out, gate_out, up_out,
    info, blk, sel, selt, sgate, snd, rows, wg, wu, wd, pg, pu, dh,
    ht, dgt, dut, dg, du, brow, trow, pw, ra, rb, given,
    in_sem, w_sem, is_sem, ir_sem, zs_sem, zr_sem, xs_sem, xr_sem,
    bs_sem, br_sem, ts_sem, tr_sem, ys_sem, ya_sem, yb_sem, ms_sem, mr_sem,
):
    dp, ex = lax.axis_index("dp"), lax.axis_index("expert")
    y, zl = lax.div(dp, 2), lax.rem(dp, 2)
    zh, xc = lax.div(ex, NE), lax.rem(ex, NE)
    sign = 1 - 2 * zl
    zh_next, zh_prev = lax.rem(zh + sign + 4, 4), lax.rem(zh - sign + 4, 4)
    y1, y2, y3 = lax.rem(y + 1, 4), lax.rem(y + 2, 4), lax.rem(y + 3, 4)

    def dev(y_, zl_, zh_, xc_):
        return (y_ * 2 + zl_, zh_ * NE + xc_)

    up = dev(y, 0, lax.rem(zh + 1, 4), xc)
    down = dev(y, 1, lax.rem(zh + 3, 4), xc)
    ahead = dev(y, zl, zh_next, xc)
    prev_same = dev(y, zl, zh_prev, xc)
    prev_other = dev(y, 1 - zl, zh_prev, xc)
    y_up = dev(y1, zl, zh, xc)
    y_down = dev(y3, zl, zh, xc)
    mate = dev(y, 1 - zl, zh, xc)

    def copy(src, dst, send, recv, where):
        return pltpu.make_async_remote_copy(
            src_ref=src, dst_ref=dst, send_sem=send, recv_sem=recv,
            device_id=where, device_id_type=MESH)

    def landed(ref, sem):
        pltpu.make_async_copy(ref, ref, sem).wait()

    def span(n, size):
        return pl.ds(pl.multiple_of(n * size, size), size)

    loads = []
    for q in range(2 * NQ):
        src = tok_in if q < NQ else cot_in
        loads.append(pltpu.make_async_copy(
            src.at[:, pl.ds(C * (q % NQ), C)], blk.at[q, 0], in_sem.at[q]))
    wloads = [pltpu.make_async_copy(a.at[0], b, w_sem.at[i])
              for i, (a, b) in enumerate(((wg_in, wg), (wu_in, wu), (wd_in, wd)))]
    barrier = pltpu.get_barrier_semaphore()
    for where in (ahead, prev_same, prev_other, y_up, y_down, mate):
        pl.semaphore_signal(barrier, inc=1, device_id=where, device_id_type=MESH)

    def greet(i, carry):
        peer = lax.rem(xc + i, NE)
        pl.semaphore_signal(barrier, inc=1, device_id=dev(y, zl, zh, peer), device_id_type=MESH)
        return carry

    lax.fori_loop(1, NE, greet, 0)
    for load in loads:
        load.start()
    for load in wloads:
        load.start()
    info[0, 0:TOP] = routes_in[...].astype(F32)
    info[0, TOP:2 * TOP] = gates_in[...]
    for load in loads:
        load.wait()
    pl.semaphore_wait(barrier, 6 + NE - 1)

    def z_copy(ref, i, send, recv):
        if i == 0:
            return copy(ref.at[0], ref.at[1 + zl], send, recv.at[zl], up)
        if i == 1:
            return copy(ref.at[0], ref.at[2 - zl], send, recv.at[1 - zl], down)
        return copy(ref.at[2], ref.at[3], send, recv.at[2], ahead)

    def block_copy(q, i):
        return z_copy(blk.at[q], i, zs_sem.at[0], zr_sem.at[q])

    def info_copy(i):
        return z_copy(info, i, is_sem.at[0], ir_sem)

    info_copy(0).start()
    info_copy(1).start()

    def send_own(q):
        block_copy(q, 0).start()
        block_copy(q, 1).start()

    for q in range(AHEAD):
        send_own(q)
    landed(info.at[2], ir_sem.at[1])
    info_copy(2).start()
    pg[...] = jnp.zeros_like(pg)
    pu[...] = jnp.zeros_like(pu)
    dh[...] = jnp.zeros_like(dh)

    def build():
        landed(info.at[1], ir_sem.at[0])
        landed(info.at[3], ir_sem.at[2])
        before_mask = (lax.broadcasted_iota(jnp.int32, (TOK, TOK), 0)
                       < lax.broadcasted_iota(jnp.int32, (TOK, TOK), 1)).astype(F32).astype(BF16)
        expert = (lax.broadcasted_iota(jnp.int32, (NE, TOK), 0) + NE * zh).astype(F32)
        slot = lax.broadcasted_iota(jnp.int32, (PAD, TOK), 0).astype(F32)
        scales = [jnp.zeros((PAD, 1), F32) for _ in range(NE)]
        for b in range(NB):
            chosen = jnp.zeros((NE, TOK), F32)
            weight = jnp.zeros((NE, TOK), F32)
            for k in range(TOP):
                hit = info[b, k:k + 1, :] == expert
                chosen = chosen + jnp.where(hit, 1.0, 0.0)
                weight = weight + jnp.where(hit, info[b, TOP + k:TOP + k + 1, :], 0.0)
            place = dot(chosen.astype(BF16), before_mask) + float(CAP * b)
            place = jnp.where(chosen > 0.0, place, -1.0)
            for j in range(NE):
                mine = jnp.where(slot == place[j:j + 1, :], 1.0, 0.0)
                sel[PAD * j:PAD * (j + 1), TOK * b:TOK * (b + 1)] = mine.astype(BF16)
                scales[j] = scales[j] + jnp.sum(mine * weight[j:j + 1, :], axis=1, keepdims=True)
        for j in range(NE):
            sgate[PAD * j:PAD * (j + 1), :] = jnp.broadcast_to(scales[j], (PAD, 128))

    def flip():
        for b in range(NB):
            at = slice(TOK * b, TOK * (b + 1))
            selt[at, :] = jnp.transpose(sel[:, at].astype(F32)).astype(BF16)

    def spread(src, dst, send, recv):
        def one(i, carry):
            peer = lax.rem(xc + i, NE)
            copy(src.at[peer], dst.at[xc], send, recv, dev(y, zl, zh, peer)).start()
            return carry

        lax.fori_loop(1, NE, one, 0)

    def pick(q):
        got = dot(sel[...], blk[q].reshape(NB * TOK, C))
        got = got * jnp.where(q >= NQ, sgate[:, 0:1], 1.0)
        snd[q] = got.astype(BF16).reshape(NE, PAD, C)
        spread(snd.at[q], rows.at[q], xs_sem.at[0], xr_sem.at[q])
        rows[q, xc] = snd[q, xc]

    def chunk_of(ref, q):
        return ref[q].reshape(ROWS, C)

    def forward(q):
        def part(n, carry):
            cols = span(n, 256)
            pg[:, cols] += dot(chunk_of(rows, q), wg[span(q, C), cols])
            pu[:, cols] += dot(chunk_of(rows, q), wu[span(q, C), cols])
            return carry

        lax.fori_loop(0, H // 256, part, 0)

    def activate():
        def part(n, carry):
            cols = span(n, 128)
            pre, mul = pg[:, cols], pu[:, cols]
            sigma = jax.nn.sigmoid(pre)
            act = pre * sigma
            ht[cols, :] = jnp.transpose(act * mul).astype(BF16)
            pg[:, cols] = act
            pu[:, cols] = mul * sigma * (1.0 + pre * (1.0 - sigma))
            return carry

        lax.fori_loop(0, H // 128, part, 0)

    def backward(q):
        def part(n, carry):
            cols = span(n, 256)
            dh[:, cols] += dot(chunk_of(rows, q), wd[cols, span(q - NQ, C)], ((1,), (1,)))
            return carry

        lax.fori_loop(0, H // 256, part, 0)

    lefts, firsts = (ht, dgt, dut), (NQ, 0, 0)

    def shares(w, g):
        def part(n, carry):
            q = g * (GC // C) + n
            got = dot(lefts[w][...], chunk_of(rows, firsts[w] + q))
            pw[w * NG + g, :, :, :, span(n, C)] = got.astype(BF16).reshape(4, 2, HZ, C)
            return carry

        lax.fori_loop(0, GC // C, part, 0)

    def ring(u, src, dst, recv, i):
        copy(src, dst, ys_sem.at[0], recv, y_down if i else y_up).start()

    def send_far(u):
        for i in range(2):
            ring(u, pw.at[u, y2, i], ra.at[u, i], ya_sem.at[u, i], i)

    def send_near(u):
        for i in range(2):
            ring(u, pw.at[u, y3 if i else y1, 1 - i], rb.at[u, i, 1 - i], yb_sem.at[u], i)

    def relay(u):
        for i in range(2):
            landed(ra.at[u, i], ya_sem.at[u, i])
            at = y3 if i else y1
            pw[u, at, i] = (pw[u, at, i].astype(F32) + ra[u, i].astype(F32)).astype(BF16)
            ring(u, pw.at[u, at, i], rb.at[u, i, i], yb_sem.at[u], i)

    def mate_copy(u):
        return copy(pw.at[u, y, 1 - zl], given.at[u], ms_sem.at[0], mr_sem.at[u], mate)

    def ring_sum(u, half):
        return (pw[u, y, half].astype(F32) + rb[u, 0, half].astype(F32)
                + rb[u, 1, half].astype(F32))

    def settle(u):
        landed(rb.at[u], yb_sem.at[u])
        pw[u, y, 1 - zl] = ring_sum(u, 1 - zl).astype(BF16)
        mate_copy(u).start()

    def finish(w, g):
        u = w * NG + g
        landed(given.at[u], mr_sem.at[u])
        total = ring_sum(u, zl) + given[u].astype(F32)
        (down_out, gate_out, up_out)[w][:, span(g, GC)] = total

    def stage(s, carry):
        @pl.when(s + AHEAD < 2 * NQ)
        def _():
            send_own(s + AHEAD)

        @pl.when(s < 2 * NQ)
        def _():
            landed(blk.at[s, 2], zr_sem.at[s, 1])
            block_copy(s, 2).start()
            landed(blk.at[s, 1], zr_sem.at[s, 0])

        @pl.when(s == 1)
        def _():
            build()

        @pl.when((s >= 1) & (s < 2 * NQ + 1))
        def _():
            landed(blk.at[s - 1, 3], zr_sem.at[s - 1, 2])
            pick(s - 1)

        @pl.when(s == 1)
        def _():
            flip()

        @pl.when(s == 3)
        def _():
            for load in wloads:
                load.wait()

        @pl.when(s >= 3)
        def _():
            q = s - 3
            landed(rows.at[q, pl.ds(0, NE - 1)], xr_sem.at[q])

            @pl.when(q < NQ)
            def _():
                forward(q)

            @pl.when(q == NQ - 1)
            def _():
                activate()

            @pl.when(q >= NQ)
            def _():
                backward(q)

            @pl.when((q > NQ) & (lax.rem(q, GC // C) == GC // C - 1))
            def _():
                g = lax.div(q - NQ, GC // C)
                shares(0, g)
                send_far(g)
                send_near(g)

                @pl.when(g >= 1)
                def _():
                    relay(g - 1)

                @pl.when(g >= 2)
                def _():
                    settle(g - 2)

        return carry

    lax.fori_loop(0, 2 * NQ + 3, stage, 0)

    def derive(n, carry):
        cols = span(n, 128)
        grad = dh[:, cols]
        d_up = grad * pg[:, cols]
        d_gate = grad * pu[:, cols]
        du[:, cols] = d_up.astype(BF16)
        dg[:, cols] = d_gate.astype(BF16)
        dut[cols, :] = jnp.transpose(d_up).astype(BF16)
        dgt[cols, :] = jnp.transpose(d_gate).astype(BF16)
        return carry

    lax.fori_loop(0, H // 128, derive, 0)

    landed(snd.at[:, pl.ds(0, NE - 1)], xs_sem.at[0])
    landed(blk.at[:, pl.ds(0, 3)], zs_sem.at[0])
    landed(info.at[pl.ds(0, 3)], is_sem.at[0])

    def back(q):
        at = span(q, C)
        got = dot(dg[...], wg[at, :], ((1,), (1,))) + dot(du[...], wu[at, :], ((1,), (1,)))
        snd[q] = got.astype(BF16).reshape(NE, PAD, C)
        spread(snd.at[q], brow.at[q], bs_sem.at[0], br_sem.at[q])
        brow[q, xc] = snd[q, xc]

    for w in (1, 2):
        def both(g, carry):
            shares(w, g)
            send_far(w * NG + g)
            back((w - 1) * NG + g)
            return carry

        lax.fori_loop(0, NG, both, 0)

    def near(u, carry):
        send_near(u)
        return carry

    lax.fori_loop(NG, NU, near, 0)

    def t_copy(q, b):
        at = 2 if b == 3 else zl
        return copy(blk.at[q, b], trow.at[q, at], ts_sem.at[0], tr_sem.at[q, at],
                    prev_other if b == 2 else prev_same)

    def own_sum(q):
        return pl.ds(pl.multiple_of(lax.rem(q, 4) * TOK, TOK), TOK), span(lax.div(q, 4), C)

    def combine(q):
        landed(brow.at[q, pl.ds(0, NE - 1)], br_sem.at[q])
        got = dot(selt[...], chunk_of(brow, q)).reshape(NB, TOK, C)
        blk[q, pl.ds(1, 3)] = got[1:].astype(BF16)
        t_copy(q, 3).start()
        t_copy(q, 1).start()
        pg[own_sum(q)] = got[0]

    def pass_on(q):
        landed(trow.at[q, 2], tr_sem.at[q, 2])
        blk[q, 2] = (blk[q, 2].astype(F32) + trow[q, 2].astype(F32)).astype(BF16)
        t_copy(q, 2).start()

    relay(NG - 1)
    settle(NG - 2)

    def return_step(q, carry):
        @pl.when(q < NQ)
        def _():
            combine(q)
            relay(NG + q)

        @pl.when(q >= 1)
        def _():
            pass_on(q - 1)

        return carry

    lax.fori_loop(0, NQ + 1, return_step, 0)
    settle(NG - 1)
    for g in range(NG):
        finish(0, g)

    def finish_tokens(q):
        landed(trow.at[q, 0], tr_sem.at[q, 0])
        landed(trow.at[q, 1], tr_sem.at[q, 1])
        total = pg[own_sum(q)] + trow[q, 0].astype(F32) + trow[q, 1].astype(F32)
        tg_out[:, span(q, C)] = total.astype(BF16)

    for w in (1, 2):
        def last(g, carry):
            settle(w * NG + g)
            finish_tokens((w - 1) * NG + g)

            @pl.when(g >= 1)
            def _():
                finish(w, g - 1)

            return carry

        lax.fori_loop(0, NG, last, 0)
        finish(w, NG - 1)

    landed(pw.at[:, pl.ds(0, 3)], ys_sem.at[0])
    landed(pw.at[:, 0, 0], ms_sem.at[0])
    landed(snd.at[pl.ds(0, NQ), pl.ds(0, NE - 1)], bs_sem.at[0])
    landed(blk.at[pl.ds(0, NQ), pl.ds(1, 3)], ts_sem.at[0])


PIECES = 2


def hand_on_kernel(*refs):
    ins, outs, held, sem_in, sem_out = refs[0:4], refs[4:8], refs[8:12], refs[12], refs[13]
    loads, stores = [], []
    for i in range(4):
        part = ins[i].shape[0] // PIECES
        for n in range(PIECES):
            at = pl.ds(n * part, part)
            loads.append(pltpu.make_async_copy(ins[i].at[at], held[i].at[at], sem_in.at[i, n]))
            stores.append(pltpu.make_async_copy(held[i].at[at], outs[i].at[at], sem_out.at[i, n]))
    for c in loads:
        c.start()
    for load, store in zip(loads, stores):
        load.wait()
        store.start()
    for c in stores:
        c.wait()


def hand_on(results):
    hbm = pl.BlockSpec(memory_space=pl.ANY)
    return pl.pallas_call(
        hand_on_kernel,
        out_shape=tuple(jax.ShapeDtypeStruct(r.shape, r.dtype) for r in results),
        in_specs=[hbm] * 4,
        out_specs=(hbm,) * 4,
        scratch_shapes=[pltpu.VMEM(r.shape, r.dtype) for r in results]
        + [pltpu.SemaphoreType.DMA((4, PIECES))] * 2,
        cost_estimate=pl.CostEstimate(
            flops=0, bytes_accessed=6 * 1024 * 1024, transcendentals=0),
    )(*results)


def body(tokens, cotangent, routes, gates, w_gate, w_up, w_down):
    hbm = pl.BlockSpec(memory_space=pl.ANY)
    vmem = pl.BlockSpec(memory_space=pltpu.VMEM)
    V, S = pltpu.VMEM, pltpu.SemaphoreType.DMA
    results = pl.pallas_call(
        kernel,
        out_shape=(
            jax.ShapeDtypeStruct((TOK, D), BF16),
            jax.ShapeDtypeStruct((HZ, D), F32),
            jax.ShapeDtypeStruct((HZ, D), F32),
            jax.ShapeDtypeStruct((HZ, D), F32),
        ),
        in_specs=[vmem, vmem, hbm, hbm, hbm, hbm, hbm],
        out_specs=(vmem, vmem, vmem, vmem),
        scratch_shapes=[
            V((NB, 2 * TOP, TOK), F32),
            V((2 * NQ, NB, TOK, C), BF16),
            V((ROWS, NB * TOK), BF16), V((NB * TOK, ROWS), BF16),
            V((ROWS, 128), F32),
            V((2 * NQ, NE, PAD, C), BF16),
            V((2 * NQ, NE, PAD, C), BF16),
            V((D, H), BF16), V((D, H), BF16), V((H, D), BF16),
            V((ROWS, H), F32), V((ROWS, H), F32), V((ROWS, H), F32),
            V((H, ROWS), BF16), V((H, ROWS), BF16), V((H, ROWS), BF16),
            V((ROWS, H), BF16), V((ROWS, H), BF16),
            V((NQ, NE, PAD, C), BF16),
            V((NQ, 3, TOK, C), BF16),
            V((NU, 4, 2, HZ, GC), BF16),
            V((NU, 2, HZ, GC), BF16),
            V((NU, 2, 2, HZ, GC), BF16),
            V((NU, HZ, GC), BF16),
            S((2 * NQ,)), S((3,)), S((1,)), S((3,)),
            S((1,)), S((2 * NQ, 3)), S((1,)), S((2 * NQ,)),
            S((1,)), S((NQ,)), S((1,)), S((NQ, 3)),
            S((1,)), S((NU, 2)), S((NU,)), S((1,)), S((NU,)),
        ],
        compiler_params=pltpu.CompilerParams(
            collective_id=0, has_side_effects=True, vmem_limit_bytes=62 * 1024 * 1024),
        cost_estimate=pl.CostEstimate(
            flops=8 * 2 * ROWS * D * H, bytes_accessed=16 * 1024 * 1024, transcendentals=ROWS * H),
    )(routes.T, gates.T, tokens, cotangent, w_gate, w_up, w_down)
    token_grad, down, gate, up = hand_on(results)
    return token_grad, gate.T[None], up.T[None], down[None]


def solution(mesh):
    rows = P(("dp", "expert"), None)
    return jax.shard_map(
        body,
        mesh=mesh,
        in_specs=(rows, rows, rows, rows) + (P("expert", None, None),) * 3,
        out_specs=(rows, P("expert", None, "dp"), P("expert", None, "dp"), P("expert", "dp", None)),
        check_vma=False,
    )
```

```python
import jax
import jax.numpy as jnp
from jax import lax
from jax.experimental import pallas as pl
from jax.experimental.pallas import tpu as pltpu
from jax.sharding import PartitionSpec as P

MESH = pl.DeviceIdType.MESH
F32 = jnp.float32
BF16 = jnp.bfloat16

D = 2048
H = 768
TOP = 4
TOK = 128
CAP = 17
NB = 4
NE = 8
PAD = 80
ROWS = NE * PAD
NQ = 8
C = D // NQ
AHEAD = 2
WINDOW = 2
LAG = 1
NG = 8
GC = D // NG
NU = 3 * NG
HY = H // 4
HZ = HY // 2


def dot(a, b, dims=((1,), (0,))):
    return lax.dot_general(a, b, (dims, ((), ())), preferred_element_type=F32)


def kernel(
    routes_in, gates_in, tok_in, cot_in, wg_in, wu_in, wd_in,
    tg_out, grads_out,
    info, blk, sel, selt, sgate, snd, rows, wg, wu, wd, pg, pu, dh,
    ht, dgt, dut, dg, du, brow, trow, pw, ra, rb, given,
    in_sem, w_sem, is_sem, ir_sem, zs_sem, zr_sem, xs_sem, xr_sem,
    bs_sem, br_sem, ts_sem, tr_sem, ys_sem, ya_sem, yb_sem, ms_sem, mr_sem,
):
    dp, ex = lax.axis_index("dp"), lax.axis_index("expert")
    y, zl = lax.div(dp, 2), lax.rem(dp, 2)
    zh, xc = lax.div(ex, NE), lax.rem(ex, NE)
    sign = 1 - 2 * zl
    zh_next, zh_prev = lax.rem(zh + sign + 4, 4), lax.rem(zh - sign + 4, 4)
    y1, y2, y3 = lax.rem(y + 1, 4), lax.rem(y + 2, 4), lax.rem(y + 3, 4)

    def dev(y_, zl_, zh_, xc_):
        return (y_ * 2 + zl_, zh_ * NE + xc_)

    up = dev(y, 0, lax.rem(zh + 1, 4), xc)
    down = dev(y, 1, lax.rem(zh + 3, 4), xc)
    ahead = dev(y, zl, zh_next, xc)
    prev_same = dev(y, zl, zh_prev, xc)
    prev_other = dev(y, 1 - zl, zh_prev, xc)
    y_up = dev(y1, zl, zh, xc)
    y_down = dev(y3, zl, zh, xc)
    mate = dev(y, 1 - zl, zh, xc)

    def copy(src, dst, send, recv, where):
        return pltpu.make_async_remote_copy(
            src_ref=src, dst_ref=dst, send_sem=send, recv_sem=recv,
            device_id=where, device_id_type=MESH)

    def landed(ref, sem):
        pltpu.make_async_copy(ref, ref, sem).wait()

    def span(n, size):
        return pl.ds(pl.multiple_of(n * size, size), size)

    loads = []
    for q in range(2 * NQ):
        src = tok_in if q < NQ else cot_in
        loads.append(pltpu.make_async_copy(
            src.at[:, pl.ds(C * (q % NQ), C)], blk.at[q, 0], in_sem.at[q]))
    wloads = [pltpu.make_async_copy(a.at[0], b, w_sem.at[i])
              for i, (a, b) in enumerate(((wg_in, wg), (wu_in, wu), (wd_in, wd)))]
    barrier = pltpu.get_barrier_semaphore()
    for where in (ahead, prev_same, prev_other, y_up, y_down, mate):
        pl.semaphore_signal(barrier, inc=1, device_id=where, device_id_type=MESH)

    def greet(i, carry):
        peer = lax.rem(xc + i, NE)
        pl.semaphore_signal(barrier, inc=1, device_id=dev(y, zl, zh, peer), device_id_type=MESH)
        return carry

    lax.fori_loop(1, NE, greet, 0)
    for load in loads:
        load.start()
    for load in wloads:
        load.start()
    info[0, 0:TOP] = routes_in[...].astype(F32)
    info[0, TOP:2 * TOP] = gates_in[...]
    for load in loads:
        load.wait()
    pl.semaphore_wait(barrier, 6 + NE - 1)

    def z_copy(ref, i, send, recv):
        if i == 0:
            return copy(ref.at[0], ref.at[1 + zl], send, recv.at[zl], up)
        if i == 1:
            return copy(ref.at[0], ref.at[2 - zl], send, recv.at[1 - zl], down)
        return copy(ref.at[2], ref.at[3], send, recv.at[2], ahead)

    def block_copy(q, i):
        return z_copy(blk.at[q], i, zs_sem.at[0], zr_sem.at[q])

    def info_copy(i):
        return z_copy(info, i, is_sem.at[0], ir_sem)

    info_copy(0).start()
    info_copy(1).start()

    def send_own(q):
        block_copy(q, 0).start()
        block_copy(q, 1).start()

    for q in range(AHEAD):
        send_own(q)
    landed(info.at[2], ir_sem.at[1])
    info_copy(2).start()
    pg[...] = jnp.zeros_like(pg)
    pu[...] = jnp.zeros_like(pu)
    dh[...] = jnp.zeros_like(dh)

    def build():
        landed(info.at[1], ir_sem.at[0])
        landed(info.at[3], ir_sem.at[2])
        before_mask = (lax.broadcasted_iota(jnp.int32, (TOK, TOK), 0)
                       < lax.broadcasted_iota(jnp.int32, (TOK, TOK), 1)).astype(F32).astype(BF16)
        expert = (lax.broadcasted_iota(jnp.int32, (NE, TOK), 0) + NE * zh).astype(F32)
        slot = lax.broadcasted_iota(jnp.int32, (PAD, TOK), 0).astype(F32)
        scales = [jnp.zeros((PAD, 1), F32) for _ in range(NE)]
        for b in range(NB):
            chosen = jnp.zeros((NE, TOK), F32)
            weight = jnp.zeros((NE, TOK), F32)
            for k in range(TOP):
                hit = info[b, k:k + 1, :] == expert
                chosen = chosen + jnp.where(hit, 1.0, 0.0)
                weight = weight + jnp.where(hit, info[b, TOP + k:TOP + k + 1, :], 0.0)
            place = dot(chosen.astype(BF16), before_mask) + float(CAP * b)
            place = jnp.where(chosen > 0.0, place, -1.0)
            for j in range(NE):
                mine = jnp.where(slot == place[j:j + 1, :], 1.0, 0.0)
                sel[PAD * j:PAD * (j + 1), TOK * b:TOK * (b + 1)] = mine.astype(BF16)
                scales[j] = scales[j] + jnp.sum(mine * weight[j:j + 1, :], axis=1, keepdims=True)
        for j in range(NE):
            sgate[PAD * j:PAD * (j + 1), :] = jnp.broadcast_to(scales[j], (PAD, 128))

    def flip():
        for b in range(NB):
            at = slice(TOK * b, TOK * (b + 1))
            selt[at, :] = jnp.transpose(sel[:, at].astype(F32)).astype(BF16)

    def spread(src, dst, send, recv):
        def one(i, carry):
            peer = lax.rem(xc + i, NE)
            copy(src.at[peer], dst.at[xc], send, recv, dev(y, zl, zh, peer)).start()
            return carry

        lax.fori_loop(1, NE, one, 0)

    def pick(q):
        got = dot(sel[...], blk[q].reshape(NB * TOK, C))
        got = got * jnp.where(q >= NQ, sgate[:, 0:1], 1.0)
        snd[q] = got.astype(BF16).reshape(NE, PAD, C)
        spread(snd.at[q], rows.at[q], xs_sem.at[0], xr_sem.at[q])
        rows[q, xc] = snd[q, xc]

    def chunk_of(ref, q):
        return ref[q].reshape(ROWS, C)

    def forward(q):
        def part(n, carry):
            cols = span(n, 256)
            pg[:, cols] += dot(chunk_of(rows, q), wg[span(q, C), cols])
            pu[:, cols] += dot(chunk_of(rows, q), wu[span(q, C), cols])
            return carry

        lax.fori_loop(0, H // 256, part, 0)

    def activate():
        def part(n, carry):
            cols = span(n, 128)
            pre, mul = pg[:, cols], pu[:, cols]
            sigma = jax.nn.sigmoid(pre)
            act = pre * sigma
            ht[cols, :] = jnp.transpose(act * mul).astype(BF16)
            pg[:, cols] = act
            pu[:, cols] = mul * sigma * (1.0 + pre * (1.0 - sigma))
            return carry

        lax.fori_loop(0, H // 128, part, 0)

    def backward(q):
        def part(n, carry):
            cols = span(n, 256)
            dh[:, cols] += dot(chunk_of(rows, q), wd[cols, span(q - NQ, C)], ((1,), (1,)))
            return carry

        lax.fori_loop(0, H // 256, part, 0)

    lefts, firsts = (ht, dgt, dut), (NQ, 0, 0)

    def shares(w, g):
        def part(n, carry):
            q = g * (GC // C) + n
            got = dot(lefts[w][...], chunk_of(rows, firsts[w] + q))
            pw[w * NG + g, :, :, :, span(n, C)] = got.astype(BF16).reshape(4, 2, HZ, C)
            return carry

        lax.fori_loop(0, GC // C, part, 0)

    def ring(u, src, dst, recv, i):
        copy(src, dst, ys_sem.at[0], recv, y_down if i else y_up).start()

    def send_far(u):
        for i in range(2):
            ring(u, pw.at[u, y2, i], ra.at[u, i], ya_sem.at[u, i], i)

    def send_near(u):
        for i in range(2):
            ring(u, pw.at[u, y3 if i else y1, 1 - i], rb.at[u, i, 1 - i], yb_sem.at[u], i)

    def relay(u):
        for i in range(2):
            landed(ra.at[u, i], ya_sem.at[u, i])
            at = y3 if i else y1
            pw[u, at, i] = (pw[u, at, i].astype(F32) + ra[u, i].astype(F32)).astype(BF16)
            ring(u, pw.at[u, at, i], rb.at[u, i, i], yb_sem.at[u], i)

    def mate_copy(u):
        return copy(pw.at[u, y, 1 - zl], given.at[u], ms_sem.at[0], mr_sem.at[u], mate)

    def ring_sum(u, half):
        return (pw[u, y, half].astype(F32) + rb[u, 0, half].astype(F32)
                + rb[u, 1, half].astype(F32))

    def settle(u):
        landed(rb.at[u], yb_sem.at[u])
        pw[u, y, 1 - zl] = ring_sum(u, 1 - zl).astype(BF16)
        mate_copy(u).start()

    def finish(u):
        w, g = lax.div(u, NG), lax.rem(u, NG)
        landed(given.at[u], mr_sem.at[u])
        total = ring_sum(u, zl) + given[u].astype(F32)
        grads_out[w, :, span(g, GC)] = total

    def stage(s, carry):
        @pl.when(s + AHEAD < 2 * NQ)
        def _():
            send_own(s + AHEAD)

        @pl.when(s < 2 * NQ)
        def _():
            landed(blk.at[s, 2], zr_sem.at[s, 1])
            block_copy(s, 2).start()
            landed(blk.at[s, 1], zr_sem.at[s, 0])

        @pl.when(s == 1)
        def _():
            build()

        @pl.when((s >= LAG) & (s < 2 * NQ + LAG))
        def _():
            landed(blk.at[s - LAG, 3], zr_sem.at[s - LAG, 2])
            pick(s - LAG)

        @pl.when(s == 1)
        def _():
            flip()

        @pl.when(s == 3)
        def _():
            for load in wloads:
                load.wait()

        @pl.when(s >= LAG + 2)
        def _():
            q = s - LAG - 2
            landed(rows.at[q, pl.ds(0, NE - 1)], xr_sem.at[q])

            @pl.when(q < NQ)
            def _():
                forward(q)

            @pl.when(q == NQ - 1)
            def _():
                activate()

            @pl.when(q >= NQ)
            def _():
                backward(q)

            @pl.when(q >= NQ)
            def _():
                g = q - NQ
                shares(0, g)
                send_far(g)
                send_near(g)

                @pl.when(g >= 1)
                def _():
                    relay(g - 1)

                @pl.when(g >= 2)
                def _():
                    settle(g - 2)

        return carry

    lax.fori_loop(0, 2 * NQ + LAG + 2, stage, 0)

    def derive(n, carry):
        cols = span(n, 128)
        grad = dh[:, cols]
        d_up = grad * pg[:, cols]
        d_gate = grad * pu[:, cols]
        du[:, cols] = d_up.astype(BF16)
        dg[:, cols] = d_gate.astype(BF16)
        dut[cols, :] = jnp.transpose(d_up).astype(BF16)
        dgt[cols, :] = jnp.transpose(d_gate).astype(BF16)
        return carry

    lax.fori_loop(0, H // 128, derive, 0)

    landed(snd.at[:, pl.ds(0, NE - 1)], xs_sem.at[0])
    landed(blk.at[:, pl.ds(0, 3)], zs_sem.at[0])
    landed(info.at[pl.ds(0, 3)], is_sem.at[0])

    def back(q):
        at = span(q, C)
        got = dot(dg[...], wg[at, :], ((1,), (1,))) + dot(du[...], wu[at, :], ((1,), (1,)))
        snd[q] = got.astype(BF16).reshape(NE, PAD, C)
        spread(snd.at[q], brow.at[q], bs_sem.at[0], br_sem.at[q])
        brow[q, xc] = snd[q, xc]

    for w in (1, 2):
        def both(g, carry):
            shares(w, g)
            send_far(w * NG + g)

            @pl.when(lax.rem(g, 2) == 0)
            def _():
                back((w - 1) * (NG // 2) + lax.div(g, 2))

            return carry

        lax.fori_loop(0, NG, both, 0)

    def t_copy(q, b):
        at = 2 if b == 3 else zl
        return copy(blk.at[q, b], trow.at[q, at], ts_sem.at[0], tr_sem.at[q, at],
                    prev_other if b == 2 else prev_same)

    def own_sum(q):
        return pl.ds(pl.multiple_of(lax.rem(q, 4) * TOK, TOK), TOK), span(lax.div(q, 4), C)

    def combine(q):
        landed(brow.at[q, pl.ds(0, NE - 1)], br_sem.at[q])
        got = dot(selt[...], chunk_of(brow, q)).reshape(NB, TOK, C)
        blk[q, pl.ds(1, 3)] = got[1:].astype(BF16)
        t_copy(q, 3).start()
        t_copy(q, 1).start()
        pg[own_sum(q)] = got[0]

    def pass_on(q):
        landed(trow.at[q, 2], tr_sem.at[q, 2])
        blk[q, 2] = (blk[q, 2].astype(F32) + trow[q, 2].astype(F32)).astype(BF16)
        t_copy(q, 2).start()

    def finish_tokens(q):
        landed(trow.at[q, 0], tr_sem.at[q, 0])
        landed(trow.at[q, 1], tr_sem.at[q, 1])
        total = pg[own_sum(q)] + trow[q, 0].astype(F32) + trow[q, 1].astype(F32)
        tg_out[:, span(q, C)] = total.astype(BF16)

    relay(NG - 1)

    def return_step(i, carry):
        @pl.when(i < NQ)
        def _():
            for n in range(2):
                send_near(NG + 2 * i + n)
                relay(NG + 2 * i + n)
            combine(i)

        @pl.when(i == 0)
        def _():
            settle(NG - 2)
            settle(NG - 1)

        @pl.when((i >= 1) & (i < NQ + 1))
        def _():
            pass_on(i - 1)
            finish(i - 1)

        @pl.when(i >= WINDOW)
        def _():
            for n in range(2):
                settle(NG + 2 * (i - WINDOW) + n)

        @pl.when(i >= WINDOW + 1)
        def _():
            finish_tokens(i - WINDOW - 1)
            for n in range(2):
                finish(NG + 2 * (i - WINDOW - 1) + n)

        return carry

    lax.fori_loop(0, NQ + WINDOW, return_step, 0)
    finish_tokens(NQ - 1)
    for n in range(2):
        finish(NU - 2 + n)

    landed(pw.at[:, pl.ds(0, 3)], ys_sem.at[0])
    landed(pw.at[:, 0, 0], ms_sem.at[0])
    landed(snd.at[pl.ds(0, NQ), pl.ds(0, NE - 1)], bs_sem.at[0])
    landed(blk.at[pl.ds(0, NQ), pl.ds(1, 3)], ts_sem.at[0])


PIECES = 2


def hand_on_kernel(*refs):
    token_in, grads_in, outs = refs[0], refs[1], refs[2:6]
    token_held, grads_held, sem_in, sem_out = refs[6:10]
    loads, stores = [], []
    for i in range(4):
        src = grads_in.at[i - 1] if i else token_in
        mid = grads_held.at[i - 1] if i else token_held
        part = src.shape[0] // PIECES
        for n in range(PIECES):
            at = pl.ds(n * part, part)
            loads.append(pltpu.make_async_copy(src.at[at], mid.at[at], sem_in.at[i, n]))
            stores.append(pltpu.make_async_copy(mid.at[at], outs[i].at[at], sem_out.at[i, n]))
    for c in loads:
        c.start()
    for load, store in zip(loads, stores):
        load.wait()
        store.start()
    for c in stores:
        c.wait()


def hand_on(results):
    hbm = pl.BlockSpec(memory_space=pl.ANY)
    return pl.pallas_call(
        hand_on_kernel,
        out_shape=(jax.ShapeDtypeStruct((TOK, D), BF16),)
        + (jax.ShapeDtypeStruct((HZ, D), F32),) * 3,
        in_specs=[hbm] * 2,
        out_specs=(hbm,) * 4,
        scratch_shapes=[pltpu.VMEM(r.shape, r.dtype) for r in results]
        + [pltpu.SemaphoreType.DMA((4, PIECES))] * 2,
        cost_estimate=pl.CostEstimate(
            flops=0, bytes_accessed=6 * 1024 * 1024, transcendentals=0),
    )(*results)


def body(tokens, cotangent, routes, gates, w_gate, w_up, w_down):
    hbm = pl.BlockSpec(memory_space=pl.ANY)
    vmem = pl.BlockSpec(memory_space=pltpu.VMEM)
    V, S = pltpu.VMEM, pltpu.SemaphoreType.DMA
    results = pl.pallas_call(
        kernel,
        out_shape=(
            jax.ShapeDtypeStruct((TOK, D), BF16),
            jax.ShapeDtypeStruct((3, HZ, D), F32),
        ),
        in_specs=[vmem, vmem, hbm, hbm, hbm, hbm, hbm],
        out_specs=(vmem, vmem),
        scratch_shapes=[
            V((NB, 2 * TOP, TOK), F32),
            V((2 * NQ, NB, TOK, C), BF16),
            V((ROWS, NB * TOK), BF16), V((NB * TOK, ROWS), BF16),
            V((ROWS, 128), F32),
            V((2 * NQ, NE, PAD, C), BF16),
            V((2 * NQ, NE, PAD, C), BF16),
            V((D, H), BF16), V((D, H), BF16), V((H, D), BF16),
            V((ROWS, H), F32), V((ROWS, H), F32), V((ROWS, H), F32),
            V((H, ROWS), BF16), V((H, ROWS), BF16), V((H, ROWS), BF16),
            V((ROWS, H), BF16), V((ROWS, H), BF16),
            V((NQ, NE, PAD, C), BF16),
            V((NQ, 3, TOK, C), BF16),
            V((NU, 4, 2, HZ, GC), BF16),
            V((NU, 2, HZ, GC), BF16),
            V((NU, 2, 2, HZ, GC), BF16),
            V((NU, HZ, GC), BF16),
            S((2 * NQ,)), S((3,)), S((1,)), S((3,)),
            S((1,)), S((2 * NQ, 3)), S((1,)), S((2 * NQ,)),
            S((1,)), S((NQ,)), S((1,)), S((NQ, 3)),
            S((1,)), S((NU, 2)), S((NU,)), S((1,)), S((NU,)),
        ],
        compiler_params=pltpu.CompilerParams(
            collective_id=0, has_side_effects=True, vmem_limit_bytes=62 * 1024 * 1024),
        cost_estimate=pl.CostEstimate(
            flops=8 * 2 * ROWS * D * H, bytes_accessed=16 * 1024 * 1024, transcendentals=ROWS * H),
    )(routes.T, gates.T, tokens, cotangent, w_gate, w_up, w_down)
    token_grad, down, gate, up = hand_on(results)
    return token_grad, gate.T[None], up.T[None], down[None]


def solution(mesh):
    rows = P(("dp", "expert"), None)
    return jax.shard_map(
        body,
        mesh=mesh,
        in_specs=(rows, rows, rows, rows) + (P("expert", None, None),) * 3,
        out_specs=(rows, P("expert", None, "dp"), P("expert", None, "dp"), P("expert", "dp", None)),
        check_vma=False,
    )
```

```python
import jax
import jax.numpy as jnp
from jax import lax
from jax.experimental import pallas as pl
from jax.experimental.pallas import tpu as pltpu
from jax.sharding import PartitionSpec as P

MESH = pl.DeviceIdType.MESH
F32 = jnp.float32
BF16 = jnp.bfloat16

D = 2048
H = 768
TOP = 4
TOK = 128
CAP = 17
NB = 4
NE = 8
PAD = 80
ROWS = NE * PAD
NQ = 8
C = D // NQ
AHEAD = 2
WINDOW = 6
COMBINE = 9
LAG = 1
NG = 8
GC = D // NG
NU = 3 * NG
HY = H // 4
HZ = HY // 2


def dot(a, b, dims=((1,), (0,))):
    return lax.dot_general(a, b, (dims, ((), ())), preferred_element_type=F32)


def kernel(
    routes_in, gates_in, tok_in, cot_in, wg_in, wu_in, wd_in,
    tg_out, grads_out,
    info, blk, sel, selt, sgate, snd, rows, wg, wu, wd, pg, pu, dh,
    ht, dgt, dut, dg, du, brow, trow, pw, ra, rb, given,
    in_sem, w_sem, is_sem, ir_sem, zs_sem, zr_sem, xs_sem, xr_sem,
    bs_sem, br_sem, ts_sem, tr_sem, ys_sem, ya_sem, yb_sem, ms_sem, mr_sem,
):
    dp, ex = lax.axis_index("dp"), lax.axis_index("expert")
    y, zl = lax.div(dp, 2), lax.rem(dp, 2)
    zh, xc = lax.div(ex, NE), lax.rem(ex, NE)
    sign = 1 - 2 * zl
    zh_next, zh_prev = lax.rem(zh + sign + 4, 4), lax.rem(zh - sign + 4, 4)
    y1, y2, y3 = lax.rem(y + 1, 4), lax.rem(y + 2, 4), lax.rem(y + 3, 4)

    def dev(y_, zl_, zh_, xc_):
        return (y_ * 2 + zl_, zh_ * NE + xc_)

    up = dev(y, 0, lax.rem(zh + 1, 4), xc)
    down = dev(y, 1, lax.rem(zh + 3, 4), xc)
    ahead = dev(y, zl, zh_next, xc)
    prev_same = dev(y, zl, zh_prev, xc)
    prev_other = dev(y, 1 - zl, zh_prev, xc)
    y_up = dev(y1, zl, zh, xc)
    y_down = dev(y3, zl, zh, xc)
    mate = dev(y, 1 - zl, zh, xc)

    def copy(src, dst, send, recv, where):
        return pltpu.make_async_remote_copy(
            src_ref=src, dst_ref=dst, send_sem=send, recv_sem=recv,
            device_id=where, device_id_type=MESH)

    def landed(ref, sem):
        pltpu.make_async_copy(ref, ref, sem).wait()

    def span(n, size):
        return pl.ds(pl.multiple_of(n * size, size), size)

    loads = []
    for q in range(2 * NQ):
        src = tok_in if q < NQ else cot_in
        loads.append(pltpu.make_async_copy(
            src.at[:, pl.ds(C * (q % NQ), C)], blk.at[q, 0], in_sem.at[q]))
    wloads = [pltpu.make_async_copy(a.at[0], b, w_sem.at[i])
              for i, (a, b) in enumerate(((wg_in, wg), (wu_in, wu), (wd_in, wd)))]
    barrier = pltpu.get_barrier_semaphore()
    for where in (ahead, prev_same, prev_other, y_up, y_down, mate):
        pl.semaphore_signal(barrier, inc=1, device_id=where, device_id_type=MESH)

    def greet(i, carry):
        peer = lax.rem(xc + i, NE)
        pl.semaphore_signal(barrier, inc=1, device_id=dev(y, zl, zh, peer), device_id_type=MESH)
        return carry

    lax.fori_loop(1, NE, greet, 0)
    for load in loads:
        load.start()
    for load in wloads:
        load.start()
    info[0, 0:TOP] = routes_in[...].astype(F32)
    info[0, TOP:2 * TOP] = gates_in[...]
    for load in loads:
        load.wait()
    pl.semaphore_wait(barrier, 6 + NE - 1)

    def z_copy(ref, i, send, recv):
        if i == 0:
            return copy(ref.at[0], ref.at[1 + zl], send, recv.at[zl], up)
        if i == 1:
            return copy(ref.at[0], ref.at[2 - zl], send, recv.at[1 - zl], down)
        return copy(ref.at[2], ref.at[3], send, recv.at[2], ahead)

    def block_copy(q, i):
        return z_copy(blk.at[q], i, zs_sem.at[0], zr_sem.at[q])

    def info_copy(i):
        return z_copy(info, i, is_sem.at[0], ir_sem)

    info_copy(0).start()
    info_copy(1).start()

    def send_own(q):
        block_copy(q, 0).start()
        block_copy(q, 1).start()

    for q in range(AHEAD):
        send_own(q)
    landed(info.at[2], ir_sem.at[1])
    info_copy(2).start()
    pg[...] = jnp.zeros_like(pg)
    pu[...] = jnp.zeros_like(pu)
    dh[...] = jnp.zeros_like(dh)

    def build():
        landed(info.at[1], ir_sem.at[0])
        landed(info.at[3], ir_sem.at[2])
        before_mask = (lax.broadcasted_iota(jnp.int32, (TOK, TOK), 0)
                       < lax.broadcasted_iota(jnp.int32, (TOK, TOK), 1)).astype(F32).astype(BF16)
        expert = (lax.broadcasted_iota(jnp.int32, (NE, TOK), 0) + NE * zh).astype(F32)
        slot = lax.broadcasted_iota(jnp.int32, (PAD, TOK), 0).astype(F32)
        scales = [jnp.zeros((PAD, 1), F32) for _ in range(NE)]
        for b in range(NB):
            chosen = jnp.zeros((NE, TOK), F32)
            weight = jnp.zeros((NE, TOK), F32)
            for k in range(TOP):
                hit = info[b, k:k + 1, :] == expert
                chosen = chosen + jnp.where(hit, 1.0, 0.0)
                weight = weight + jnp.where(hit, info[b, TOP + k:TOP + k + 1, :], 0.0)
            place = dot(chosen.astype(BF16), before_mask) + float(CAP * b)
            place = jnp.where(chosen > 0.0, place, -1.0)
            for j in range(NE):
                mine = jnp.where(slot == place[j:j + 1, :], 1.0, 0.0)
                sel[PAD * j:PAD * (j + 1), TOK * b:TOK * (b + 1)] = mine.astype(BF16)
                scales[j] = scales[j] + jnp.sum(mine * weight[j:j + 1, :], axis=1, keepdims=True)
        for j in range(NE):
            sgate[PAD * j:PAD * (j + 1), :] = jnp.broadcast_to(scales[j], (PAD, 128))

    def flip():
        for b in range(NB):
            at = slice(TOK * b, TOK * (b + 1))
            selt[at, :] = jnp.transpose(sel[:, at].astype(F32)).astype(BF16)

    def spread(src, dst, send, recv):
        def one(i, carry):
            peer = lax.rem(xc + i, NE)
            copy(src.at[peer], dst.at[xc], send, recv, dev(y, zl, zh, peer)).start()
            return carry

        lax.fori_loop(1, NE, one, 0)

    def pick(q):
        got = dot(sel[...], blk[q].reshape(NB * TOK, C))
        got = got * jnp.where(q >= NQ, sgate[:, 0:1], 1.0)
        snd[q] = got.astype(BF16).reshape(NE, PAD, C)
        spread(snd.at[q], rows.at[q], xs_sem.at[0], xr_sem.at[q])
        rows[q, xc] = snd[q, xc]

    def chunk_of(ref, q):
        return ref[q].reshape(ROWS, C)

    def forward(q):
        def part(n, carry):
            cols = span(n, 256)
            pg[:, cols] += dot(chunk_of(rows, q), wg[span(q, C), cols])
            pu[:, cols] += dot(chunk_of(rows, q), wu[span(q, C), cols])
            return carry

        lax.fori_loop(0, H // 256, part, 0)

    def activate():
        def part(n, carry):
            cols = span(n, 128)
            pre, mul = pg[:, cols], pu[:, cols]
            sigma = jax.nn.sigmoid(pre)
            act = pre * sigma
            ht[cols, :] = jnp.transpose(act * mul).astype(BF16)
            pg[:, cols] = act
            pu[:, cols] = mul * sigma * (1.0 + pre * (1.0 - sigma))
            return carry

        lax.fori_loop(0, H // 128, part, 0)

    def backward(q):
        def part(n, carry):
            cols = span(n, 256)
            dh[:, cols] += dot(chunk_of(rows, q), wd[cols, span(q - NQ, C)], ((1,), (1,)))
            return carry

        lax.fori_loop(0, H // 256, part, 0)

    lefts, firsts = (ht, dgt, dut), (NQ, 0, 0)

    def shares(w, g):
        def part(n, carry):
            q = g * (GC // C) + n
            got = dot(lefts[w][...], chunk_of(rows, firsts[w] + q))
            pw[w * NG + g, :, :, :, span(n, C)] = got.astype(BF16).reshape(4, 2, HZ, C)
            return carry

        lax.fori_loop(0, GC // C, part, 0)

    def ring(u, src, dst, recv, i):
        copy(src, dst, ys_sem.at[0], recv, y_down if i else y_up).start()

    def send_far(u):
        for i in range(2):
            ring(u, pw.at[u, y2, i], ra.at[u, i], ya_sem.at[u, i], i)

    def send_near(u):
        for i in range(2):
            ring(u, pw.at[u, y3 if i else y1, 1 - i], rb.at[u, i, 1 - i], yb_sem.at[u], i)

    def relay(u):
        for i in range(2):
            landed(ra.at[u, i], ya_sem.at[u, i])
            at = y3 if i else y1
            pw[u, at, i] = (pw[u, at, i].astype(F32) + ra[u, i].astype(F32)).astype(BF16)
            ring(u, pw.at[u, at, i], rb.at[u, i, i], yb_sem.at[u], i)

    def mate_copy(u):
        return copy(pw.at[u, y, 1 - zl], given.at[u], ms_sem.at[0], mr_sem.at[u], mate)

    def ring_sum(u, half):
        return (pw[u, y, half].astype(F32) + rb[u, 0, half].astype(F32)
                + rb[u, 1, half].astype(F32))

    def settle(u):
        landed(rb.at[u], yb_sem.at[u])
        pw[u, y, 1 - zl] = ring_sum(u, 1 - zl).astype(BF16)
        mate_copy(u).start()

    def finish(u):
        w, g = lax.div(u, NG), lax.rem(u, NG)
        landed(given.at[u], mr_sem.at[u])
        total = ring_sum(u, zl) + given[u].astype(F32)
        grads_out[w, :, span(g, GC)] = total

    def stage(s, carry):
        @pl.when(s + AHEAD < 2 * NQ)
        def _():
            send_own(s + AHEAD)

        @pl.when(s < 2 * NQ)
        def _():
            landed(blk.at[s, 2], zr_sem.at[s, 1])
            block_copy(s, 2).start()
            landed(blk.at[s, 1], zr_sem.at[s, 0])

        @pl.when(s == 1)
        def _():
            build()

        @pl.when((s >= LAG) & (s < 2 * NQ + LAG))
        def _():
            landed(blk.at[s - LAG, 3], zr_sem.at[s - LAG, 2])
            pick(s - LAG)

        @pl.when(s == 1)
        def _():
            flip()

        @pl.when(s == 3)
        def _():
            for load in wloads:
                load.wait()

        @pl.when(s >= LAG + 2)
        def _():
            q = s - LAG - 2
            landed(rows.at[q, pl.ds(0, NE - 1)], xr_sem.at[q])

            @pl.when(q < NQ)
            def _():
                forward(q)

            @pl.when(q == NQ - 1)
            def _():
                activate()

            @pl.when(q >= NQ)
            def _():
                backward(q)

            @pl.when(q >= NQ)
            def _():
                g = q - NQ
                shares(0, g)
                send_far(g)
                send_near(g)

                @pl.when(g >= 1)
                def _():
                    relay(g - 1)

                @pl.when(g >= 2)
                def _():
                    settle(g - 2)

        return carry

    lax.fori_loop(0, 2 * NQ + LAG + 2, stage, 0)

    def derive(factor, flat, turned):
        def part(n, carry):
            cols = span(n, 128)
            grad = dh[:, cols] * factor[:, cols]
            flat[:, cols] = grad.astype(BF16)
            turned[cols, :] = jnp.transpose(grad).astype(BF16)
            return carry

        lax.fori_loop(0, H // 128, part, 0)

    derive(pu, dg, dgt)
    for g in range(2):
        shares(1, g)
        send_far(NG + g)
    derive(pg, du, dut)

    landed(snd.at[:, pl.ds(0, NE - 1)], xs_sem.at[0])
    landed(blk.at[:, pl.ds(0, 3)], zs_sem.at[0])
    landed(info.at[pl.ds(0, 3)], is_sem.at[0])

    def back(q):
        at = span(q, C)
        got = dot(dg[...], wg[at, :], ((1,), (1,))) + dot(du[...], wu[at, :], ((1,), (1,)))
        snd[q] = got.astype(BF16).reshape(NE, PAD, C)
        spread(snd.at[q], brow.at[q], bs_sem.at[0], br_sem.at[q])
        brow[q, xc] = snd[q, xc]

    def t_copy(q, b):
        at = 2 if b == 3 else zl
        return copy(blk.at[q, b], trow.at[q, at], ts_sem.at[0], tr_sem.at[q, at],
                    prev_other if b == 2 else prev_same)

    def own_sum(q):
        return pl.ds(pl.multiple_of(lax.rem(q, 4) * TOK, TOK), TOK), span(lax.div(q, 4), C)

    def combine(q):
        landed(brow.at[q, pl.ds(0, NE - 1)], br_sem.at[q])
        got = dot(selt[...], chunk_of(brow, q)).reshape(NB, TOK, C)
        blk[q, pl.ds(1, 3)] = got[1:].astype(BF16)
        t_copy(q, 3).start()
        t_copy(q, 1).start()
        pg[own_sum(q)] = got[0]

    def pass_on(q):
        landed(trow.at[q, 2], tr_sem.at[q, 2])
        blk[q, 2] = (blk[q, 2].astype(F32) + trow[q, 2].astype(F32)).astype(BF16)
        t_copy(q, 2).start()

    def finish_tokens(q):
        landed(trow.at[q, 0], tr_sem.at[q, 0])
        landed(trow.at[q, 1], tr_sem.at[q, 1])
        total = pg[own_sum(q)] + trow[q, 0].astype(F32) + trow[q, 1].astype(F32)
        tg_out[:, span(q, C)] = total.astype(BF16)

    def push(u):
        send_near(u)
        relay(u)

    def mixed_step(w, g, carry):
        it = (w - 1) * NG + g
        shares(w, g)
        send_far(w * NG + g)

        @pl.when(it >= 2 * NG - WINDOW)
        def _():
            push(NG + it - (2 * NG - WINDOW))

        @pl.when(it < NQ + 2)
        def _():
            back(it - 2)

        @pl.when((it >= COMBINE) & (lax.rem(it - COMBINE, 2) == 0))
        def _():
            combine(lax.div(it - COMBINE, 2))

        @pl.when((it >= COMBINE + 4) & (lax.rem(it - COMBINE, 2) == 0))
        def _():
            pass_on(lax.div(it - COMBINE - 4, 2))

        return carry

    lax.fori_loop(2, NG, lambda g, c: mixed_step(1, g, c), 0)
    relay(NG - 1)
    settle(NG - 2)
    lax.fori_loop(0, NG, lambda g, c: mixed_step(2, g, c), 0)
    settle(NG - 1)
    summed, passed = (2 * NG + 1 - COMBINE) // 2, (2 * NG - 3 - COMBINE) // 2

    def return_step(i, carry):
        @pl.when(2 * i < 2 * NG - WINDOW)
        def _():
            for n in range(2):
                push(NG + WINDOW + 2 * i + n)

        @pl.when(i < NQ - summed)
        def _():
            combine(summed + i)

        @pl.when(i < NQ - passed)
        def _():
            pass_on(passed + i)

        for n in range(2):
            settle(NG + 2 * i + n)

        finish(i)

        @pl.when(i >= 1)
        def _():
            for n in range(2):
                finish(NG + 2 * (i - 1) + n)
            finish_tokens(i - 1)

        return carry

    lax.fori_loop(0, NG, return_step, 0)
    finish_tokens(NQ - 1)
    for n in range(2):
        finish(NU - 2 + n)

    landed(pw.at[:, pl.ds(0, 3)], ys_sem.at[0])
    landed(pw.at[:, 0, 0], ms_sem.at[0])
    landed(snd.at[pl.ds(0, NQ), pl.ds(0, NE - 1)], bs_sem.at[0])
    landed(blk.at[pl.ds(0, NQ), pl.ds(1, 3)], ts_sem.at[0])


PIECES = 2


def hand_on_kernel(*refs):
    token_in, grads_in, outs = refs[0], refs[1], refs[2:6]
    token_held, grads_held, sem_in, sem_out = refs[6:10]
    loads, stores = [], []
    for i in range(4):
        src = grads_in.at[i - 1] if i else token_in
        mid = grads_held.at[i - 1] if i else token_held
        part = src.shape[0] // PIECES
        for n in range(PIECES):
            at = pl.ds(n * part, part)
            loads.append(pltpu.make_async_copy(src.at[at], mid.at[at], sem_in.at[i, n]))
            stores.append(pltpu.make_async_copy(mid.at[at], outs[i].at[at], sem_out.at[i, n]))
    for c in loads:
        c.start()
    for load, store in zip(loads, stores):
        load.wait()
        store.start()
    for c in stores:
        c.wait()


def hand_on(results):
    hbm = pl.BlockSpec(memory_space=pl.ANY)
    return pl.pallas_call(
        hand_on_kernel,
        out_shape=(jax.ShapeDtypeStruct((TOK, D), BF16),)
        + (jax.ShapeDtypeStruct((HZ, D), F32),) * 3,
        in_specs=[hbm] * 2,
        out_specs=(hbm,) * 4,
        scratch_shapes=[pltpu.VMEM(r.shape, r.dtype) for r in results]
        + [pltpu.SemaphoreType.DMA((4, PIECES))] * 2,
        cost_estimate=pl.CostEstimate(
            flops=0, bytes_accessed=6 * 1024 * 1024, transcendentals=0),
    )(*results)


def body(tokens, cotangent, routes, gates, w_gate, w_up, w_down):
    hbm = pl.BlockSpec(memory_space=pl.ANY)
    vmem = pl.BlockSpec(memory_space=pltpu.VMEM)
    V, S = pltpu.VMEM, pltpu.SemaphoreType.DMA
    results = pl.pallas_call(
        kernel,
        out_shape=(
            jax.ShapeDtypeStruct((TOK, D), BF16),
            jax.ShapeDtypeStruct((3, HZ, D), F32),
        ),
        in_specs=[vmem, vmem, hbm, hbm, hbm, hbm, hbm],
        out_specs=(vmem, vmem),
        scratch_shapes=[
            V((NB, 2 * TOP, TOK), F32),
            V((2 * NQ, NB, TOK, C), BF16),
            V((ROWS, NB * TOK), BF16), V((NB * TOK, ROWS), BF16),
            V((ROWS, 128), F32),
            V((2 * NQ, NE, PAD, C), BF16),
            V((2 * NQ, NE, PAD, C), BF16),
            V((D, H), BF16), V((D, H), BF16), V((H, D), BF16),
            V((ROWS, H), F32), V((ROWS, H), F32), V((ROWS, H), F32),
            V((H, ROWS), BF16), V((H, ROWS), BF16), V((H, ROWS), BF16),
            V((ROWS, H), BF16), V((ROWS, H), BF16),
            V((NQ, NE, PAD, C), BF16),
            V((NQ, 3, TOK, C), BF16),
            V((NU, 4, 2, HZ, GC), BF16),
            V((NU, 2, HZ, GC), BF16),
            V((NU, 2, 2, HZ, GC), BF16),
            V((NU, HZ, GC), BF16),
            S((2 * NQ,)), S((3,)), S((1,)), S((3,)),
            S((1,)), S((2 * NQ, 3)), S((1,)), S((2 * NQ,)),
            S((1,)), S((NQ,)), S((1,)), S((NQ, 3)),
            S((1,)), S((NU, 2)), S((NU,)), S((1,)), S((NU,)),
        ],
        compiler_params=pltpu.CompilerParams(
            collective_id=0, has_side_effects=True, vmem_limit_bytes=62 * 1024 * 1024),
        cost_estimate=pl.CostEstimate(
            flops=8 * 2 * ROWS * D * H, bytes_accessed=16 * 1024 * 1024, transcendentals=ROWS * H),
    )(routes.T, gates.T, tokens, cotangent, w_gate, w_up, w_down)
    token_grad, down, gate, up = hand_on(results)
    return token_grad, gate.T[None], up.T[None], down[None]


def solution(mesh):
    rows = P(("dp", "expert"), None)
    return jax.shard_map(
        body,
        mesh=mesh,
        in_specs=(rows, rows, rows, rows) + (P("expert", None, None),) * 3,
        out_specs=(rows, P("expert", None, "dp"), P("expert", None, "dp"), P("expert", "dp", None)),
        check_vma=False,
    )
```
